32 devices in a mesh: dom: 16 (over z, y, x), sub: 2 (over core).
Axes of the slice: x: 2, y: 2, z: 4, core: 2. Of those that a mesh axis runs over, the one named last changes fastest.
Arguments:
- coupling: bfloat16 [16, 2, 16, 8, 128, 256], P('dom', 'sub'), as said below
- null_vector: bfloat16 [16, 2, 16, 128], P('dom', 'sub'), may hold values from 0.5 to 2
- aggregate_ids: int32 [16, 2, 16, 128], P('dom', 'sub'), may hold values from 0 to 31, as said below
- send_list: int32 [16, 16, 2], P('dom'), may hold values from -1 to 15, as said below
- recv_list: int32 [16, 16, 8], P('dom'), may hold values from 0 to 47, as said below
Outputs:
- coarse_tiles: float32 [256, 32, 256], P('dom', 'sub')
The draws below stay inside these ranges and needn't reach their ends.
Inputs may be any that keep to these rules, and one draw needn't show every extreme that they name: `aggregate_ids`: within each coarse block (both halves together) every aggregate id 0 to 31 is used by at least one fine row. The neighbours of partition d are the six partitions d + 1, d - 1, d + 2, d - 2, d + 4, d - 4 modulo 16. Each neighbour p of d fills all 2 slots of send_list[p, d]; every other entry is -1. Each filled slot is named by one or more entries of recv_list[d]. recv_list[d, b, 0] = b; for k = 1 to 3 it is another block of partition d (not b); for k = 4 to 7 it is 16 + p * 2 + c for a neighbour p of d, the four neighbours of one block row distinct. coupling[d, s, b, 0, i, s * 128 + i] lies between 2 and 4.
All inputs are finite; a program needn't handle non-finite values.
Results may differ from the reference program's by a relative error of at most 0.0061.
Values may be sent and summed in bfloat16 or wider, within the bound.
A program may use at most 64 MiB of HBM per device.

```python
import math
import jax
import jax.numpy as jnp
from jax import lax

ROWS = 128
AGGS = 32
NEIGH = 8
SLOTS = 2
BLOCKS = 16
N_DOM = 16
N_SUB = 2


def route_tables():
    offsets = jnp.array([1, -1, 2, -2, 4, -4], jnp.int32)
    rows = jnp.arange(BLOCKS, dtype=jnp.int32)
    ranks = jnp.arange(4, dtype=jnp.int32)
    which = (rows[:, None] + ranks[None, :]) % 6
    owners = jnp.arange(N_DOM, dtype=jnp.int32)[:, None, None]
    peers = (owners + offsets[which][None, :, :] + N_DOM) % N_DOM
    slots = jnp.broadcast_to((rows % SLOTS)[None, :, None], peers.shape)
    return (peers.astype(jnp.int32), slots.astype(jnp.int32))


def draw_send_list(key, part):
    key = jax.random.fold_in(key, 3)
    peers, slots = route_tables()
    blocks = jax.random.randint(key, (N_DOM, N_DOM, SLOTS), 0, BLOCKS).astype(jnp.int32)
    targets = jnp.broadcast_to(jnp.arange(N_DOM, dtype=jnp.int32)[:, None, None], peers.shape)
    empty = jnp.full((N_DOM, N_DOM, SLOTS), -1, jnp.int32)
    return empty.at[peers, targets, slots].set(blocks[peers, targets, slots])


def draw_recv_list(key, part):
    key = jax.random.fold_in(key, 5)
    peers, slots = route_tables()
    rows = jnp.arange(BLOCKS, dtype=jnp.int32)[None, :, None]
    steps_away = jax.random.randint(key, (N_DOM, BLOCKS, 3), 0, BLOCKS - 1).astype(jnp.int32)
    local = (rows + 1 + steps_away) % BLOCKS
    remote = BLOCKS + peers * SLOTS + slots
    diagonal = jnp.broadcast_to(rows, (N_DOM, BLOCKS, 1))
    return jnp.concatenate([diagonal, local, remote], axis=2).astype(jnp.int32)


def draw_aggregate_ids(key, part):
    key = jax.random.fold_in(key, 7)
    span_cols = N_SUB * ROWS

    def one_block(sub_key):
        order = jax.random.permutation(jax.random.fold_in(sub_key, 1), span_cols)
        extra = jax.random.randint(jax.random.fold_in(sub_key, 2), (span_cols,), 0, AGGS)
        counter = jnp.arange(span_cols, dtype=jnp.int32)
        labels = jnp.where(counter < AGGS, counter, extra).astype(jnp.int32)
        return jnp.zeros((span_cols,), jnp.int32).at[order].set(labels)
    keys = jax.random.split(key, N_DOM * BLOCKS)
    ids = jax.vmap(one_block)(keys).reshape(N_DOM, BLOCKS, N_SUB, ROWS)
    return jnp.transpose(ids, (0, 2, 1, 3))


def draw_coupling(key, part):
    key = jax.random.fold_in(key, 11)
    shape = (N_DOM, N_SUB, BLOCKS, NEIGH, ROWS, N_SUB * ROWS)
    first = jax.random.fold_in(key, 1)
    second = jax.random.fold_in(key, 2)
    values = 0.25 * jax.random.normal(first, shape, jnp.float32)
    diag = jax.random.uniform(second, (N_DOM, N_SUB, BLOCKS, 1, ROWS, 1), jnp.float32, 2.0, 4.0)
    sub_pos = jnp.arange(N_SUB).reshape(1, N_SUB, 1, 1, 1, 1)
    slot_pos = jnp.arange(NEIGH).reshape(1, 1, 1, NEIGH, 1, 1)
    row_pos = jnp.arange(ROWS).reshape(1, 1, 1, 1, ROWS, 1)
    col_pos = jnp.arange(N_SUB * ROWS).reshape(1, 1, 1, 1, 1, N_SUB * ROWS)
    on_diag = (slot_pos == 0) & (col_pos == sub_pos * ROWS + row_pos)
    return jnp.where(on_diag, diag, values).astype(jnp.bfloat16)


def level_of(rng, shape, cuts, least, largest):
    level, own = 1.0, jax.random.fold_in(rng, 6)
    for axis_at, parts in cuts:
        draws = jnp.exp(jax.random.uniform(jax.random.fold_in(own, axis_at), (parts,), jnp.float32, least / len(cuts), largest / len(cuts)))
        level = level * jnp.repeat(draws, shape[axis_at] // parts).reshape([-1 if axis == axis_at else 1 for axis in range(len(shape))])
    return level


def setup_inputs(seed: int = 0) -> dict:
    streams_of = jax.random.split(jax.random.key(seed), 6)
    coupling = draw_coupling(jax.random.fold_in(streams_of[5], 71), 0)
    null_vector = jnp.clip(jnp.exp(math.log(2.0) - 1.3862944 * jax.random.uniform(streams_of[1], (N_DOM, N_SUB, BLOCKS, ROWS), jnp.float32) ** level_of(streams_of[1], (N_DOM, N_SUB, BLOCKS, ROWS), ((0, 16), (1, 2)), -0.2, 0.2)), 0.5, 2.0).astype(jnp.bfloat16)
    aggregate_ids = draw_aggregate_ids(jax.random.fold_in(streams_of[5], 71), 0)
    send_list = draw_send_list(jax.random.fold_in(streams_of[5], 71), 0)
    recv_list = draw_recv_list(jax.random.fold_in(streams_of[5], 71), 0)
    return dict(coupling=coupling, null_vector=null_vector, aggregate_ids=aggregate_ids, send_list=send_list, recv_list=recv_list)


OMEGA = 0.6666667
HIGH = lax.Precision.HIGHEST

def reference(coupling, null_vector, aggregate_ids, send_list, recv_list):
    span_cols = N_SUB * ROWS
    labels = jnp.arange(AGGS, dtype=jnp.int32)
    scattered = jnp.where(aggregate_ids[:, :, :, None, :] == labels[:, None], null_vector[:, :, :, None, :], jnp.zeros((), jnp.bfloat16))
    gathered = jnp.transpose(scattered, (0, 2, 3, 1, 4)).reshape(N_DOM, BLOCKS, AGGS, span_cols).astype(jnp.float32)
    tentative = (gathered / jnp.sqrt(lax.optimization_barrier(jnp.sum(gathered * gathered, axis=-1, keepdims=True)))).astype(jnp.bfloat16)

    def smooth_one(items):
        tiles_part, tent_part = items
        tent_wide = tent_part.astype(jnp.float32)
        halves = []
        for sub_index in range(N_SUB):
            tile = tiles_part[sub_index, :, 0].astype(jnp.float32)
            own_rows = tent_wide[:, :, sub_index * ROWS:(sub_index + 1) * ROWS]
            diag_vals = jnp.diagonal(tile[:, :, sub_index * ROWS:(sub_index + 1) * ROWS], axis1=1, axis2=2)
            smoothing = jnp.einsum('bgj,bij->bgi', tent_wide, tile, precision=HIGH)
            halves.append((own_rows - OMEGA * smoothing / diag_vals[:, None, :]).astype(jnp.bfloat16))
        return jnp.stack(halves, 0)
    smoothed = lax.map(smooth_one, (coupling, tentative))
    prolong = jnp.transpose(smoothed, (0, 2, 3, 1, 4)).reshape(N_DOM, BLOCKS, AGGS, span_cols)
    is_local = recv_list < BLOCKS
    remote = jnp.maximum(recv_list - BLOCKS, 0)
    source = (remote // SLOTS).astype(jnp.int32)
    slot_index = (remote % SLOTS).astype(jnp.int32)
    target = jnp.arange(N_DOM, dtype=jnp.int32)[:, None, None]
    remote_block = send_list[source, jnp.broadcast_to(target, source.shape), slot_index]
    part_index = jnp.where(is_local, jnp.broadcast_to(target, source.shape), source).astype(jnp.int32)
    block_index = jnp.where(is_local, recv_list, remote_block).astype(jnp.int32)

    def galerkin(items):
        tiles_part, smooth_part, parts_row, blocks_row = items
        partner = prolong[parts_row, blocks_row].astype(jnp.float32)
        total = jnp.zeros((BLOCKS, AGGS, NEIGH, AGGS), jnp.float32)
        for sub_index in range(N_SUB):
            left_part = jnp.einsum('bgi,bkij->bkgj', smooth_part[sub_index].astype(jnp.float32), tiles_part[sub_index].astype(jnp.float32), precision=HIGH).astype(jnp.bfloat16)
            total = total + jnp.einsum('bkgj,bkhj->bgkh', left_part.astype(jnp.float32), partner, precision=HIGH)
        return total.reshape(BLOCKS, AGGS, NEIGH * AGGS)
    coarse = lax.map(galerkin, (coupling, smoothed, part_index, block_index))
    paired = coarse.reshape(N_DOM // 2, 2, 2, BLOCKS // 2, AGGS, NEIGH * AGGS)
    return jnp.transpose(paired, (0, 2, 1, 3, 4, 5)).reshape(N_DOM * BLOCKS, AGGS, NEIGH * AGGS)
```

```python
import functools

import jax
import jax.numpy as jnp
from jax import lax
from jax.experimental import pallas as pl
from jax.experimental.pallas import tpu as pltpu
from jax.sharding import PartitionSpec as P

AGGS = 32
OMEGA = 0.6666667
OFFSETS = (1, -1, 2, -2, 4, -4)
GROUP = 4
MESH = pl.DeviceIdType.MESH
NT = (((1,), (1,)), ((), ()))
NN = (((1,), (0,)), ((), ()))


def kernel(
    domains,
    null_ref,
    ids_ref,
    send_ref,
    recv_ref,
    c_hbm,
    out_ref,
    c_vmem,
    null_full,
    null_other,
    ids_full,
    sm_ref,
    pro_local,
    pro_remote,
    send_buf,
    left_ref,
    keep,
    xs_send,
    xs_recv,
    dom_send,
    dom_recv,
    table,
    load_sem,
    pair_sems,
    sm_sems,
    far_send_sems,
    far_recv_sems,
    xs_send_sems,
    xs_recv_sems,
    dom_send_sems,
    dom_recv_sems,
):
    blocks, neigh, rows, cols = c_hbm.shape
    half = blocks // 2
    groups = blocks // GROUP
    near = neigh // 2
    slots = send_ref.shape[1]
    me = lax.axis_index("dom")
    sub = lax.axis_index("sub")
    other = 1 - sub
    parity = lax.rem(me, 2)
    mate = me + 1 - 2 * parity
    first = half * (1 - parity)
    own_lanes = pl.ds(pl.multiple_of(sub * rows, rows), rows)
    other_lanes = pl.ds(pl.multiple_of(other * rows, rows), rows)
    is_low = sub == 0

    def group_start(group):
        return lax.rem(group * GROUP + first, blocks)

    diag_load = pltpu.make_async_copy(c_hbm.at[:, 0], c_vmem.at[:, 0], load_sem.at[groups])
    diag_load.start()

    def tile_load(group):
        span = pl.ds(group_start(group), GROUP)
        rest = pl.ds(1, neigh - 1)
        return pltpu.make_async_copy(
            c_hbm.at[span, rest], c_vmem.at[span, rest], load_sem.at[group]
        )

    for group in range(groups):
        tile_load(group).start()

    barrier = pltpu.get_barrier_semaphore()
    targets = [lax.rem(me + offset + domains, domains) for offset in OFFSETS]
    pl.semaphore_signal(barrier, inc=1, device_id=(me, other), device_id_type=MESH)
    for target in targets:
        for core in range(2):
            pl.semaphore_signal(barrier, inc=1, device_id=(target, core), device_id_type=MESH)

    null_full[:, own_lanes] = null_ref[...].astype(jnp.float32)
    ids_full[:, own_lanes] = ids_ref[...]

    def clear(place, carry):
        table[place] = 0
        return carry

    lax.fori_loop(0, domains * slots, clear, 0)
    for position, offset in enumerate(OFFSETS):
        source = lax.rem(me - offset + domains, domains)
        for slot in range(slots):
            table[source * slots + slot] = position * slots + slot

    pl.semaphore_wait(barrier, 1 + 2 * len(OFFSETS))

    null_copy = pltpu.make_async_remote_copy(
        null_ref, null_other, pair_sems.at[0], pair_sems.at[1], (me, other), MESH
    )
    ids_copy = pltpu.make_async_remote_copy(
        ids_ref, ids_full.at[:, own_lanes], pair_sems.at[2], pair_sems.at[3], (me, other), MESH
    )
    null_copy.start()
    ids_copy.start()
    diag_load.wait()
    null_copy.wait_recv()
    ids_copy.wait_recv()
    null_full[:, other_lanes] = null_other[...].astype(jnp.float32)

    labels = lax.broadcasted_iota(jnp.int32, (AGGS, cols), 0)
    on_diag = lax.broadcasted_iota(jnp.int32, (rows, rows), 0) == lax.broadcasted_iota(
        jnp.int32, (rows, rows), 1
    )

    def smooth_group(group, carry):
        for step in range(GROUP):
            block = group * GROUP + step
            values = null_full[pl.ds(block, 1), :]
            aggregate = ids_full[pl.ds(block, 1), :]
            scattered = jnp.where(aggregate == labels, values, 0.0)
            norm = jnp.sum(scattered * scattered, axis=1, keepdims=True)
            tentative = (scattered / jnp.sqrt(norm)).astype(jnp.bfloat16)
            wide = tentative.astype(jnp.float32)
            own = jnp.where(is_low, wide[:, :rows], wide[:, rows:])
            square = c_vmem[block, 0, :, own_lanes].astype(jnp.float32)
            diag = jnp.sum(jnp.where(on_diag, square, 0.0), axis=0, keepdims=True)
            smoothing = lax.dot_general(
                tentative, c_vmem[block, 0], NT, preferred_element_type=jnp.float32
            )
            smoothed = (own - smoothing * (OMEGA / diag)).astype(jnp.bfloat16)
            sm_ref[block] = smoothed
            pro_local[block, :, own_lanes] = smoothed
        return carry

    lax.fori_loop(0, groups, smooth_group, 0)

    sm_copy = pltpu.make_async_remote_copy(
        sm_ref, pro_local.at[:, :, own_lanes], sm_sems.at[0], sm_sems.at[1], (me, other), MESH
    )
    sm_copy.start()
    far_copies = []
    for position, target in enumerate(targets):
        for slot in range(slots):
            chosen = jnp.clip(send_ref[target, slot], 0, blocks - 1)
            send_buf[position, slot] = sm_ref[chosen]
        for core in range(2):
            copy = pltpu.make_async_remote_copy(
                send_buf.at[position],
                pro_remote.at[pl.ds(position * slots, slots), :, own_lanes],
                far_send_sems.at[position, core],
                far_recv_sems.at[position, sub],
                (target, core),
                MESH,
            )
            copy.start()
            far_copies.append(copy)

    def left_group(group, carry):
        tile_load(group).wait()
        for step in range(GROUP):
            block = group_start(group) + step
            smoothed = sm_ref[block]
            for tile in range(neigh):
                left = lax.dot_general(
                    smoothed, c_vmem[block, tile], NN, preferred_element_type=jnp.float32
                )
                left_ref[block, tile * AGGS : (tile + 1) * AGGS, :] = left.astype(jnp.bfloat16)
        return carry

    lax.fori_loop(0, groups, left_group, 0)

    sm_copy.wait_recv()
    for position, target in enumerate(targets):
        for core in range(2):
            pltpu.make_async_remote_copy(
                send_buf.at[position],
                pro_remote.at[
                    pl.ds(position * slots, slots), :, pl.ds(core * rows, rows)
                ],
                far_send_sems.at[position, core],
                far_recv_sems.at[position, core],
                (target, core),
                MESH,
            ).wait_recv()

    lane_tile = lax.broadcasted_iota(jnp.int32, (AGGS, near * AGGS), 1) // AGGS

    def tiles_of(left, partners):
        full = lax.dot_general(
            left, jnp.concatenate(partners, axis=0), NT, preferred_element_type=jnp.float32
        )
        picked = full[:AGGS]
        for tile in range(1, near):
            picked = jnp.where(lane_tile == tile, full[tile * AGGS : (tile + 1) * AGGS], picked)
        return picked

    cut = AGGS // 2

    def xs_copy(group):
        span = pl.ds(group * GROUP, GROUP)
        return pltpu.make_async_remote_copy(
            xs_send.at[span],
            xs_recv.at[span],
            xs_send_sems.at[group],
            xs_recv_sems.at[group],
            (me, other),
            MESH,
        )

    def dom_copy(group):
        span = pl.ds(group * GROUP, GROUP)
        return pltpu.make_async_remote_copy(
            dom_send.at[span],
            dom_recv.at[span],
            dom_send_sems.at[group],
            dom_recv_sems.at[group],
            (mate, sub),
            MESH,
        )

    def coarse_group(group):
        for step in range(GROUP):
            block = group_start(group) + step
            place = group * GROUP + step
            local = [pro_local[block]] + [
                pro_local[recv_ref[block, tile]] for tile in range(1, near)
            ]
            remote = [
                pro_remote[table[jnp.maximum(recv_ref[block, tile] - blocks, 0)]]
                for tile in range(near, neigh)
            ]
            width = near * AGGS
            for at, part in (
                (0, tiles_of(left_ref[block, :width, :], local)),
                (width, tiles_of(left_ref[block, width:, :], remote)),
            ):
                low, high = part[:cut], part[cut:]
                keep[place, :, at : at + width] = jnp.where(is_low, low, high)
                xs_send[place, :, at : at + width] = jnp.where(is_low, high, low).astype(
                    jnp.bfloat16
                )
        xs_copy(group).start()

    def total_of(group):
        xs_copy(group).wait_recv()
        span = pl.ds(group * GROUP, GROUP)
        return keep[span] + xs_recv[span].astype(jnp.float32)

    given = groups // 2

    def given_step(group, carry):
        coarse_group(group)
        return carry

    def kept_step(group, carry):
        coarse_group(group)
        done = group - given
        dom_send[pl.ds(done * GROUP, GROUP)] = total_of(done).astype(jnp.bfloat16)
        dom_copy(done).start()
        return carry

    lax.fori_loop(0, given, given_step, 0)
    lax.fori_loop(given, groups, kept_step, 0)

    def finish_kept(group, carry):
        place = pl.multiple_of(half * parity + (group - given) * GROUP, GROUP)
        out_ref[pl.ds(place, GROUP)] = total_of(group)
        return carry

    lax.fori_loop(given, groups, finish_kept, 0)

    def finish_given(group, carry):
        dom_copy(group).wait_recv()
        place = pl.multiple_of(first + group * GROUP, GROUP)
        out_ref[pl.ds(place, GROUP)] = dom_recv[pl.ds(group * GROUP, GROUP)].astype(jnp.float32)
        return carry

    lax.fori_loop(0, given, finish_given, 0)

    null_copy.wait_send()
    ids_copy.wait_send()
    sm_copy.wait_send()
    for copy in far_copies:
        copy.wait_send()
    for group in range(groups):
        xs_copy(group).wait_send()
    for group in range(given):
        dom_copy(group).wait_send()


def per_device(coupling, null_vector, aggregate_ids, send_list, recv_list):
    tiles = coupling[0, 0]
    blocks, neigh, rows, cols = tiles.shape
    domains = lax.axis_size("dom")
    slots = send_list.shape[2]
    half = blocks // 2
    groups = blocks // GROUP
    far = len(OFFSETS)
    bf16, f32, i32 = jnp.bfloat16, jnp.float32, jnp.int32
    vmem = pl.BlockSpec(memory_space=pltpu.VMEM)
    smem = pl.BlockSpec(memory_space=pltpu.SMEM)
    dma = pltpu.SemaphoreType.DMA
    return pl.pallas_call(
        functools.partial(kernel, domains),
        out_shape=jax.ShapeDtypeStruct((blocks, AGGS // 2, neigh * AGGS), f32),
        in_specs=[vmem, vmem, smem, smem, pl.BlockSpec(memory_space=pl.ANY)],
        out_specs=vmem,
        scratch_shapes=[
            pltpu.VMEM((blocks, neigh, rows, cols), bf16),
            pltpu.VMEM((blocks, cols), f32),
            pltpu.VMEM((blocks, rows), bf16),
            pltpu.VMEM((blocks, cols), i32),
            pltpu.VMEM((blocks, AGGS, rows), bf16),
            pltpu.VMEM((blocks, AGGS, cols), bf16),
            pltpu.VMEM((far * slots, AGGS, cols), bf16),
            pltpu.VMEM((far, slots, AGGS, rows), bf16),
            pltpu.VMEM((blocks, neigh * AGGS, cols), bf16),
            pltpu.VMEM((blocks, AGGS // 2, neigh * AGGS), f32),
            pltpu.VMEM((blocks, AGGS // 2, neigh * AGGS), bf16),
            pltpu.VMEM((blocks, AGGS // 2, neigh * AGGS), bf16),
            pltpu.VMEM((half, AGGS // 2, neigh * AGGS), bf16),
            pltpu.VMEM((half, AGGS // 2, neigh * AGGS), bf16),
            pltpu.SMEM((domains * slots,), i32),
            dma((groups + 1,)),
            dma((4,)),
            dma((2,)),
            dma((far, 2)),
            dma((far, 2)),
            dma((groups,)),
            dma((groups,)),
            dma((groups // 2,)),
            dma((groups // 2,)),
        ],
        compiler_params=pltpu.CompilerParams(
            collective_id=0, has_side_effects=True, vmem_limit_bytes=48 * 1024 * 1024
        ),
    )(null_vector[0, 0], aggregate_ids[0, 0], send_list[0], recv_list[0], tiles)


def solution(mesh):
    in_specs = (
        P("dom", "sub", None, None, None, None),
        P("dom", "sub", None, None),
        P("dom", "sub", None, None),
        P("dom", None, None),
        P("dom", None, None),
    )
    out_specs = P("dom", "sub", None)
    return jax.shard_map(
        per_device, mesh=mesh, in_specs=in_specs, out_specs=out_specs, check_vma=False
    )
```

```python
import functools

import jax
import jax.numpy as jnp
from jax import lax
from jax.experimental import pallas as pl
from jax.experimental.pallas import tpu as pltpu
from jax.sharding import PartitionSpec as P

AGGS = 32
OMEGA = 0.6666667
OFFSETS = (1, -1, 2, -2, 4, -4)
GROUP = 4
MESH = pl.DeviceIdType.MESH
NT = (((1,), (1,)), ((), ()))
NN = (((1,), (0,)), ((), ()))


def kernel(
    domains,
    null_hbm,
    ids_hbm,
    send_hbm,
    recv_hbm,
    c_hbm,
    out_ref,
    null_ref,
    ids_ref,
    send_ref,
    recv_ref,
    c_vmem,
    null_full,
    null_other,
    ids_full,
    sm_ref,
    pro_local,
    pro_remote,
    send_buf,
    left_ref,
    keep,
    xs_send,
    xs_recv,
    dom_send,
    dom_recv,
    table,
    load_sem,
    small_sems,
    pair_sems,
    sm_sems,
    far_send_sems,
    far_recv_sems,
    xs_send_sems,
    xs_recv_sems,
    dom_send_sems,
    dom_recv_sems,
):
    blocks, neigh, rows, cols = c_hbm.shape
    half = blocks // 2
    groups = blocks // GROUP
    near = neigh // 2
    slots = send_hbm.shape[0]
    me = lax.axis_index("dom")
    sub = lax.axis_index("sub")
    other = 1 - sub
    parity = lax.rem(me, 2)
    mate = me + 1 - 2 * parity
    first = half * (1 - parity)
    own_lanes = pl.ds(pl.multiple_of(sub * rows, rows), rows)
    other_lanes = pl.ds(pl.multiple_of(other * rows, rows), rows)
    is_low = sub == 0

    def group_start(group):
        return lax.rem(group * GROUP + first, blocks)

    small_loads = [
        pltpu.make_async_copy(source, target, small_sems.at[place])
        for place, (source, target) in enumerate(
            (
                (null_hbm, null_ref),
                (ids_hbm, ids_ref),
                (send_hbm, send_ref),
                (recv_hbm, recv_ref),
            )
        )
    ]
    for load in small_loads:
        load.start()
    diag_load = pltpu.make_async_copy(c_hbm.at[:, 0], c_vmem.at[:, 0], load_sem.at[groups])
    diag_load.start()

    def tile_load(group):
        span = pl.ds(group_start(group), GROUP)
        rest = pl.ds(1, neigh - 1)
        return pltpu.make_async_copy(
            c_hbm.at[span, rest], c_vmem.at[span, rest], load_sem.at[group]
        )

    for group in range(groups):
        tile_load(group).start()

    barrier = pltpu.get_barrier_semaphore()
    targets = [lax.rem(me + offset + domains, domains) for offset in OFFSETS]
    pl.semaphore_signal(barrier, inc=1, device_id=(me, other), device_id_type=MESH)
    for target in targets:
        for core in range(2):
            pl.semaphore_signal(barrier, inc=1, device_id=(target, core), device_id_type=MESH)

    small_loads[0].wait()
    small_loads[1].wait()
    null_full[:, own_lanes] = null_ref[...].astype(jnp.float32)
    ids_full[:, own_lanes] = ids_ref[...]

    def clear(place, carry):
        table[place] = 0
        return carry

    lax.fori_loop(0, domains * slots, clear, 0)
    for position, offset in enumerate(OFFSETS):
        source = lax.rem(me - offset + domains, domains)
        for slot in range(slots):
            table[source * slots + slot] = position * slots + slot

    pl.semaphore_wait(barrier, 1 + 2 * len(OFFSETS))

    null_copy = pltpu.make_async_remote_copy(
        null_ref, null_other, pair_sems.at[0], pair_sems.at[1], (me, other), MESH
    )
    ids_copy = pltpu.make_async_remote_copy(
        ids_ref, ids_full.at[:, own_lanes], pair_sems.at[2], pair_sems.at[3], (me, other), MESH
    )
    null_copy.start()
    ids_copy.start()
    diag_load.wait()
    null_copy.wait_recv()
    ids_copy.wait_recv()
    null_full[:, other_lanes] = null_other[...].astype(jnp.float32)

    labels = lax.broadcasted_iota(jnp.int32, (AGGS, cols), 0)
    on_diag = lax.broadcasted_iota(jnp.int32, (rows, rows), 0) == lax.broadcasted_iota(
        jnp.int32, (rows, rows), 1
    )

    def smooth_group(group, carry):
        for step in range(GROUP):
            block = group * GROUP + step
            values = null_full[pl.ds(block, 1), :]
            aggregate = ids_full[pl.ds(block, 1), :]
            scattered = jnp.where(aggregate == labels, values, 0.0)
            norm = jnp.sum(scattered * scattered, axis=1, keepdims=True)
            tentative = (scattered / jnp.sqrt(norm)).astype(jnp.bfloat16)
            wide = tentative.astype(jnp.float32)
            own = jnp.where(is_low, wide[:, :rows], wide[:, rows:])
            square = c_vmem[block, 0, :, own_lanes].astype(jnp.float32)
            diag = jnp.sum(jnp.where(on_diag, square, 0.0), axis=0, keepdims=True)
            smoothing = lax.dot_general(
                tentative, c_vmem[block, 0], NT, preferred_element_type=jnp.float32
            )
            smoothed = (own - smoothing * (OMEGA / diag)).astype(jnp.bfloat16)
            sm_ref[block] = smoothed
            pro_local[block, :, own_lanes] = smoothed
        return carry

    lax.fori_loop(0, groups, smooth_group, 0)

    sm_copy = pltpu.make_async_remote_copy(
        sm_ref, pro_local.at[:, :, own_lanes], sm_sems.at[0], sm_sems.at[1], (me, other), MESH
    )
    sm_copy.start()
    small_loads[2].wait()
    small_loads[3].wait()
    far_copies = []
    for position, target in enumerate(targets):
        for slot in range(slots):
            chosen = jnp.clip(send_ref[slot, target], 0, blocks - 1)
            send_buf[position, slot] = sm_ref[chosen]
        for core in range(2):
            copy = pltpu.make_async_remote_copy(
                send_buf.at[position],
                pro_remote.at[pl.ds(position * slots, slots), :, own_lanes],
                far_send_sems.at[position, core],
                far_recv_sems.at[position, sub],
                (target, core),
                MESH,
            )
            copy.start()
            far_copies.append(copy)

    def left_group(group, carry):
        tile_load(group).wait()
        for step in range(GROUP):
            block = group_start(group) + step
            smoothed = sm_ref[block]
            for tile in range(neigh):
                left = lax.dot_general(
                    smoothed, c_vmem[block, tile], NN, preferred_element_type=jnp.float32
                )
                left_ref[block, tile * AGGS : (tile + 1) * AGGS, :] = left.astype(jnp.bfloat16)
        return carry

    lax.fori_loop(0, groups, left_group, 0)

    sm_copy.wait_recv()

    lane_tile = lax.broadcasted_iota(jnp.int32, (AGGS, near * AGGS), 1) // AGGS

    def tiles_of(left, partners):
        full = lax.dot_general(
            left, jnp.concatenate(partners, axis=0), NT, preferred_element_type=jnp.float32
        )
        picked = full[:AGGS]
        for tile in range(1, near):
            picked = jnp.where(lane_tile == tile, full[tile * AGGS : (tile + 1) * AGGS], picked)
        return picked

    cut = AGGS // 2

    def xs_copy(part, group):
        span = pl.ds(group * GROUP, GROUP)
        return pltpu.make_async_remote_copy(
            xs_send.at[part, span],
            xs_recv.at[part, span],
            xs_send_sems.at[part, group],
            xs_recv_sems.at[part, group],
            (me, other),
            MESH,
        )

    def dom_copy(part, group):
        span = pl.ds(group * GROUP, GROUP)
        return pltpu.make_async_remote_copy(
            dom_send.at[part, span],
            dom_recv.at[part, span],
            dom_send_sems.at[part, group],
            dom_recv_sems.at[part, group],
            (mate, sub),
            MESH,
        )

    width = near * AGGS

    def coarse_group(part, group):
        for step in range(GROUP):
            block = group_start(group) + step
            place = group * GROUP + step
            if part == 0:
                partners = [pro_local[block]] + [
                    pro_local[recv_ref[tile, block]] for tile in range(1, near)
                ]
            else:
                partners = [
                    pro_remote[table[jnp.maximum(recv_ref[tile, block] - blocks, 0)]]
                    for tile in range(near, neigh)
                ]
            tiles = tiles_of(left_ref[block, part * width : (part + 1) * width, :], partners)
            low, high = tiles[:cut], tiles[cut:]
            keep[part, place] = jnp.where(is_low, low, high)
            xs_send[part, place] = jnp.where(is_low, high, low).astype(jnp.bfloat16)
        xs_copy(part, group).start()

    def total_of(part, group):
        xs_copy(part, group).wait_recv()
        span = pl.ds(group * GROUP, GROUP)
        return keep[part, span] + xs_recv[part, span].astype(jnp.float32)

    given = groups // 2

    def column_part(part):
        def given_step(group, carry):
            coarse_group(part, group)
            return carry

        def kept_step(group, carry):
            coarse_group(part, group)
            done = group - given
            dom_send[part, pl.ds(done * GROUP, GROUP)] = total_of(part, done).astype(jnp.bfloat16)
            dom_copy(part, done).start()
            return carry

        lax.fori_loop(0, given, given_step, 0)
        lax.fori_loop(given, groups, kept_step, 0)

    def finish_part(part):
        columns = slice(part * width, (part + 1) * width)

        def finish_kept(group, carry):
            place = half * parity + (group - given) * GROUP
            out_ref[pl.ds(place, GROUP), :, columns] = total_of(part, group)
            return carry

        def finish_given(group, carry):
            dom_copy(part, group).wait_recv()
            place = first + group * GROUP
            out_ref[pl.ds(place, GROUP), :, columns] = dom_recv[
                part, pl.ds(group * GROUP, GROUP)
            ].astype(jnp.float32)
            return carry

        lax.fori_loop(given, groups, finish_kept, 0)
        return finish_given

    column_part(0)

    for position, target in enumerate(targets):
        for core in range(2):
            pltpu.make_async_remote_copy(
                send_buf.at[position],
                pro_remote.at[
                    pl.ds(position * slots, slots), :, pl.ds(core * rows, rows)
                ],
                far_send_sems.at[position, core],
                far_recv_sems.at[position, core],
                (target, core),
                MESH,
            ).wait_recv()
    column_part(1)
    finish_local = finish_part(0)
    lax.fori_loop(0, given, finish_local, 0)
    finish_remote = finish_part(1)
    lax.fori_loop(0, given, finish_remote, 0)

    null_copy.wait_send()
    ids_copy.wait_send()
    sm_copy.wait_send()
    for copy in far_copies:
        copy.wait_send()
    for part in range(2):
        for group in range(groups):
            xs_copy(part, group).wait_send()
        for group in range(given):
            dom_copy(part, group).wait_send()


def per_device(coupling, null_vector, aggregate_ids, send_list, recv_list):
    tiles = coupling[0, 0]
    blocks, neigh, rows, cols = tiles.shape
    domains = lax.axis_size("dom")
    slots = send_list.shape[2]
    half = blocks // 2
    groups = blocks // GROUP
    far = len(OFFSETS)
    bf16, f32, i32 = jnp.bfloat16, jnp.float32, jnp.int32
    hbm = pl.BlockSpec(memory_space=pltpu.HBM)
    dma = pltpu.SemaphoreType.DMA
    return pl.pallas_call(
        functools.partial(kernel, domains),
        out_shape=jax.ShapeDtypeStruct((blocks, AGGS // 2, neigh * AGGS), f32),
        in_specs=[hbm] * 5,
        out_specs=pl.BlockSpec(memory_space=pltpu.VMEM),
        scratch_shapes=[
            pltpu.VMEM((blocks, rows), bf16),
            pltpu.VMEM((blocks, rows), i32),
            pltpu.SMEM((slots, domains), i32),
            pltpu.SMEM((neigh, blocks), i32),
            pltpu.VMEM((blocks, neigh, rows, cols), bf16),
            pltpu.VMEM((blocks, cols), f32),
            pltpu.VMEM((blocks, rows), bf16),
            pltpu.VMEM((blocks, cols), i32),
            pltpu.VMEM((blocks, AGGS, rows), bf16),
            pltpu.VMEM((blocks, AGGS, cols), bf16),
            pltpu.VMEM((far * slots, AGGS, cols), bf16),
            pltpu.VMEM((far, slots, AGGS, rows), bf16),
            pltpu.VMEM((blocks, neigh * AGGS, cols), bf16),
            pltpu.VMEM((2, blocks, AGGS // 2, neigh // 2 * AGGS), f32),
            pltpu.VMEM((2, blocks, AGGS // 2, neigh // 2 * AGGS), bf16),
            pltpu.VMEM((2, blocks, AGGS // 2, neigh // 2 * AGGS), bf16),
            pltpu.VMEM((2, half, AGGS // 2, neigh // 2 * AGGS), bf16),
            pltpu.VMEM((2, half, AGGS // 2, neigh // 2 * AGGS), bf16),
            pltpu.SMEM((domains * slots,), i32),
            dma((groups + 1,)),
            dma((4,)),
            dma((4,)),
            dma((2,)),
            dma((far, 2)),
            dma((far, 2)),
            dma((2, groups)),
            dma((2, groups)),
            dma((2, groups // 2)),
            dma((2, groups // 2)),
        ],
        compiler_params=pltpu.CompilerParams(
            collective_id=0, has_side_effects=True, vmem_limit_bytes=64 * 1024 * 1024
        ),
    )(null_vector[0, 0], aggregate_ids[0, 0], send_list[0].T, recv_list[0].T, tiles)


def solution(mesh):
    in_specs = (
        P("dom", "sub", None, None, None, None),
        P("dom", "sub", None, None),
        P("dom", "sub", None, None),
        P("dom", None, None),
        P("dom", None, None),
    )
    out_specs = P("dom", "sub", None)
    return jax.shard_map(
        per_device, mesh=mesh, in_specs=in_specs, out_specs=out_specs, check_vma=False
    )
```

```python
import functools

import jax
import jax.numpy as jnp
from jax import lax
from jax.experimental import pallas as pl
from jax.experimental.pallas import tpu as pltpu
from jax.sharding import PartitionSpec as P

AGGS = 32
OMEGA = 0.6666667
OFFSETS = (1, -1, 2, -2, 4, -4)
GROUP = 4
MESH = pl.DeviceIdType.MESH
NT = (((1,), (1,)), ((), ()))
NN = (((1,), (0,)), ((), ()))


def kernel(
    domains,
    null_hbm,
    ids_hbm,
    send_hbm,
    recv_hbm,
    c_hbm,
    out_ref,
    null_ref,
    ids_ref,
    send_ref,
    recv_ref,
    c_vmem,
    null_full,
    null_other,
    ids_full,
    sm_ref,
    pro_local,
    pro_remote,
    send_buf,
    left_ref,
    keep,
    xs_send,
    xs_recv,
    dom_send,
    dom_recv,
    table,
    load_sem,
    small_sems,
    pair_sems,
    sm_sems,
    far_send_sems,
    far_recv_sems,
    xs_send_sems,
    xs_recv_sems,
    dom_send_sems,
    dom_recv_sems,
):
    blocks, neigh, rows, cols = c_hbm.shape
    half = blocks // 2
    groups = blocks // GROUP
    near = neigh // 2
    slots = send_hbm.shape[0]
    me = lax.axis_index("dom")
    sub = lax.axis_index("sub")
    other = 1 - sub
    parity = lax.rem(me, 2)
    mate = me + 1 - 2 * parity
    first = half * (1 - parity)
    own_lanes = pl.ds(pl.multiple_of(sub * rows, rows), rows)
    other_lanes = pl.ds(pl.multiple_of(other * rows, rows), rows)
    is_low = sub == 0

    def group_start(group):
        return lax.rem(group * GROUP + first, blocks)

    small_loads = [
        pltpu.make_async_copy(source, target, small_sems.at[place])
        for place, (source, target) in enumerate(
            (
                (null_hbm, null_ref),
                (ids_hbm, ids_ref),
                (send_hbm, send_ref),
                (recv_hbm, recv_ref),
            )
        )
    ]
    for load in small_loads:
        load.start()
    diag_load = pltpu.make_async_copy(c_hbm.at[:, 0], c_vmem.at[:, 0], load_sem.at[groups])
    diag_load.start()

    def tile_load(group):
        span = pl.ds(group_start(group), GROUP)
        rest = pl.ds(1, neigh - 1)
        return pltpu.make_async_copy(
            c_hbm.at[span, rest], c_vmem.at[span, rest], load_sem.at[group]
        )

    for group in range(groups):
        tile_load(group).start()

    barrier = pltpu.get_barrier_semaphore()
    targets = [lax.rem(me + offset + domains, domains) for offset in OFFSETS]
    pl.semaphore_signal(barrier, inc=1, device_id=(me, other), device_id_type=MESH)
    for target in targets:
        for core in range(2):
            pl.semaphore_signal(barrier, inc=1, device_id=(target, core), device_id_type=MESH)

    small_loads[0].wait()
    small_loads[1].wait()
    null_full[:, own_lanes] = null_ref[...].astype(jnp.float32)
    ids_full[:, own_lanes] = ids_ref[...]

    def clear(place, carry):
        table[place] = 0
        return carry

    lax.fori_loop(0, domains * slots, clear, 0)
    for position, offset in enumerate(OFFSETS):
        source = lax.rem(me - offset + domains, domains)
        for slot in range(slots):
            table[source * slots + slot] = position * slots + slot

    pl.semaphore_wait(barrier, 1 + 2 * len(OFFSETS))

    null_copy = pltpu.make_async_remote_copy(
        null_ref, null_other, pair_sems.at[0], pair_sems.at[1], (me, other), MESH
    )
    ids_copy = pltpu.make_async_remote_copy(
        ids_ref, ids_full.at[:, own_lanes], pair_sems.at[2], pair_sems.at[3], (me, other), MESH
    )
    null_copy.start()
    ids_copy.start()
    diag_load.wait()
    null_copy.wait_recv()
    ids_copy.wait_recv()
    null_full[:, other_lanes] = null_other[...].astype(jnp.float32)

    labels = lax.broadcasted_iota(jnp.int32, (AGGS, cols), 0)
    on_diag = lax.broadcasted_iota(jnp.int32, (rows, rows), 0) == lax.broadcasted_iota(
        jnp.int32, (rows, rows), 1
    )

    def smooth_group(group, carry):
        for step in range(GROUP):
            block = group * GROUP + step
            values = null_full[pl.ds(block, 1), :]
            aggregate = ids_full[pl.ds(block, 1), :]
            scattered = jnp.where(aggregate == labels, values, 0.0)
            norm = jnp.sum(scattered * scattered, axis=1, keepdims=True)
            tentative = (scattered / jnp.sqrt(norm)).astype(jnp.bfloat16)
            wide = tentative.astype(jnp.float32)
            own = jnp.where(is_low, wide[:, :rows], wide[:, rows:])
            square = c_vmem[block, 0, :, own_lanes].astype(jnp.float32)
            diag = jnp.sum(jnp.where(on_diag, square, 0.0), axis=0, keepdims=True)
            smoothing = lax.dot_general(
                tentative, c_vmem[block, 0], NT, preferred_element_type=jnp.float32
            )
            smoothed = (own - smoothing * (OMEGA / diag)).astype(jnp.bfloat16)
            sm_ref[block] = smoothed
            pro_local[block, :, own_lanes] = smoothed
        return carry

    lax.fori_loop(0, groups, smooth_group, 0)

    sm_copy = pltpu.make_async_remote_copy(
        sm_ref, pro_local.at[:, :, own_lanes], sm_sems.at[0], sm_sems.at[1], (me, other), MESH
    )
    sm_copy.start()
    small_loads[2].wait()
    small_loads[3].wait()
    far_copies = []
    for position, target in enumerate(targets):
        for slot in range(slots):
            chosen = jnp.clip(send_ref[slot, target], 0, blocks - 1)
            send_buf[position, slot] = sm_ref[chosen]
        for core in range(2):
            copy = pltpu.make_async_remote_copy(
                send_buf.at[position],
                pro_remote.at[pl.ds(position * slots, slots), :, own_lanes],
                far_send_sems.at[position, core],
                far_recv_sems.at[position, sub],
                (target, core),
                MESH,
            )
            copy.start()
            far_copies.append(copy)

    def left_group(group, carry):
        tile_load(group).wait()
        for step in range(GROUP):
            block = group_start(group) + step
            smoothed = sm_ref[block]
            for tile in range(neigh):
                left = lax.dot_general(
                    smoothed, c_vmem[block, tile], NN, preferred_element_type=jnp.float32
                )
                left_ref[block, tile * AGGS : (tile + 1) * AGGS, :] = left.astype(jnp.bfloat16)
        return carry

    lax.fori_loop(0, groups, left_group, 0)

    sm_copy.wait_recv()

    lane_tile = lax.broadcasted_iota(jnp.int32, (AGGS, near * AGGS), 1) // AGGS

    def tiles_of(left, partners):
        full = lax.dot_general(
            left, jnp.concatenate(partners, axis=0), NT, preferred_element_type=jnp.float32
        )
        picked = full[:AGGS]
        for tile in range(1, near):
            picked = jnp.where(lane_tile == tile, full[tile * AGGS : (tile + 1) * AGGS], picked)
        return picked

    cut = AGGS // 2

    def xs_copy(part, group):
        span = pl.ds(group * GROUP, GROUP)
        return pltpu.make_async_remote_copy(
            xs_send.at[part, span],
            xs_recv.at[part, span],
            xs_send_sems.at[part, group],
            xs_recv_sems.at[part, group],
            (me, other),
            MESH,
        )

    def dom_copy(part, group):
        span = pl.ds(group * GROUP, GROUP)
        return pltpu.make_async_remote_copy(
            dom_send.at[part, span],
            dom_recv.at[part, span],
            dom_send_sems.at[part, group],
            dom_recv_sems.at[part, group],
            (mate, sub),
            MESH,
        )

    width = near * AGGS

    def coarse_group(part, group):
        for step in range(GROUP):
            block = group_start(group) + step
            place = group * GROUP + step
            if part == 0:
                partners = [pro_local[block]] + [
                    pro_local[recv_ref[tile, block]] for tile in range(1, near)
                ]
            else:
                partners = [
                    pro_remote[table[jnp.maximum(recv_ref[tile, block] - blocks, 0)]]
                    for tile in range(near, neigh)
                ]
            tiles = tiles_of(left_ref[block, part * width : (part + 1) * width, :], partners)
            low, high = tiles[:cut], tiles[cut:]
            keep[part, place] = jnp.where(is_low, low, high)
            xs_send[part, place] = jnp.where(is_low, high, low).astype(jnp.bfloat16)
        xs_copy(part, group).start()

    def total_of(part, group):
        xs_copy(part, group).wait_recv()
        span = pl.ds(group * GROUP, GROUP)
        return keep[part, span] + xs_recv[part, span].astype(jnp.float32)

    given = groups // 2

    def column_part(part):
        def given_step(group, carry):
            coarse_group(part, group)
            return carry

        def kept_step(group, carry):
            coarse_group(part, group)
            done = group - given
            dom_send[part, pl.ds(done * GROUP, GROUP)] = total_of(part, done).astype(jnp.bfloat16)
            dom_copy(part, done).start()
            return carry

        lax.fori_loop(0, given, given_step, 0)
        lax.fori_loop(given, groups, kept_step, 0)

    def finish_part(part):
        columns = slice(part * width, (part + 1) * width)

        def finish_kept(group, carry):
            place = half * parity + (group - given) * GROUP
            out_ref[pl.ds(place, GROUP), :, columns] = total_of(part, group)
            return carry

        def finish_given(group, carry):
            dom_copy(part, group).wait_recv()
            place = first + group * GROUP
            out_ref[pl.ds(place, GROUP), :, columns] = dom_recv[
                part, pl.ds(group * GROUP, GROUP)
            ].astype(jnp.float32)
            return carry

        lax.fori_loop(given, groups, finish_kept, 0)
        return finish_given

    column_part(0)
    finish_local = finish_part(0)
    lax.fori_loop(0, given, finish_local, 0)

    for position, target in enumerate(targets):
        for core in range(2):
            pltpu.make_async_remote_copy(
                send_buf.at[position],
                pro_remote.at[
                    pl.ds(position * slots, slots), :, pl.ds(core * rows, rows)
                ],
                far_send_sems.at[position, core],
                far_recv_sems.at[position, core],
                (target, core),
                MESH,
            ).wait_recv()
    column_part(1)
    finish_remote = finish_part(1)
    lax.fori_loop(0, given, finish_remote, 0)

    null_copy.wait_send()
    ids_copy.wait_send()
    sm_copy.wait_send()
    for copy in far_copies:
        copy.wait_send()
    for part in range(2):
        for group in range(groups):
            xs_copy(part, group).wait_send()
        for group in range(given):
            dom_copy(part, group).wait_send()


def per_device(coupling, null_vector, aggregate_ids, send_list, recv_list):
    tiles = coupling[0, 0]
    blocks, neigh, rows, cols = tiles.shape
    domains = lax.axis_size("dom")
    slots = send_list.shape[2]
    half = blocks // 2
    groups = blocks // GROUP
    far = len(OFFSETS)
    bf16, f32, i32 = jnp.bfloat16, jnp.float32, jnp.int32
    hbm = pl.BlockSpec(memory_space=pltpu.HBM)
    dma = pltpu.SemaphoreType.DMA
    return pl.pallas_call(
        functools.partial(kernel, domains),
        out_shape=jax.ShapeDtypeStruct((blocks, AGGS // 2, neigh * AGGS), f32),
        in_specs=[hbm] * 5,
        out_specs=pl.BlockSpec(memory_space=pltpu.VMEM),
        scratch_shapes=[
            pltpu.VMEM((blocks, rows), bf16),
            pltpu.VMEM((blocks, rows), i32),
            pltpu.SMEM((slots, domains), i32),
            pltpu.SMEM((neigh, blocks), i32),
            pltpu.VMEM((blocks, neigh, rows, cols), bf16),
            pltpu.VMEM((blocks, cols), f32),
            pltpu.VMEM((blocks, rows), bf16),
            pltpu.VMEM((blocks, cols), i32),
            pltpu.VMEM((blocks, AGGS, rows), bf16),
            pltpu.VMEM((blocks, AGGS, cols), bf16),
            pltpu.VMEM((far * slots, AGGS, cols), bf16),
            pltpu.VMEM((far, slots, AGGS, rows), bf16),
            pltpu.VMEM((blocks, neigh * AGGS, cols), bf16),
            pltpu.VMEM((2, blocks, AGGS // 2, neigh // 2 * AGGS), f32),
            pltpu.VMEM((2, blocks, AGGS // 2, neigh // 2 * AGGS), bf16),
            pltpu.VMEM((2, blocks, AGGS // 2, neigh // 2 * AGGS), bf16),
            pltpu.VMEM((2, half, AGGS // 2, neigh // 2 * AGGS), bf16),
            pltpu.VMEM((2, half, AGGS // 2, neigh // 2 * AGGS), bf16),
            pltpu.SMEM((domains * slots,), i32),
            dma((groups + 1,)),
            dma((4,)),
            dma((4,)),
            dma((2,)),
            dma((far, 2)),
            dma((far, 2)),
            dma((2, groups)),
            dma((2, groups)),
            dma((2, groups // 2)),
            dma((2, groups // 2)),
        ],
        compiler_params=pltpu.CompilerParams(
            collective_id=0, has_side_effects=True, vmem_limit_bytes=64 * 1024 * 1024
        ),
    )(null_vector[0, 0], aggregate_ids[0, 0], send_list[0].T, recv_list[0].T, tiles)


def solution(mesh):
    in_specs = (
        P("dom", "sub", None, None, None, None),
        P("dom", "sub", None, None),
        P("dom", "sub", None, None),
        P("dom", None, None),
        P("dom", None, None),
    )
    out_specs = P("dom", "sub", None)
    return jax.shard_map(
        per_device, mesh=mesh, in_specs=in_specs, out_specs=out_specs, check_vma=False
    )
```
